32 devices in a mesh: rep: 2 (over y), ep: 16 (over z, x, core).
Axes of the slice: x: 2, y: 2, z: 4, core: 2. Of those that a mesh axis runs over, the one named last changes fastest.
Arguments:
- signal: bfloat16 [2048, 4096], P('ep', 'rep'), may hold values from -6 to 6
- routes: int32 [2048, 8], P('ep'), may hold values from 0 to 15, all different within a row; in each aligned block of 128 rows (0 to 127, 128 to 255, ...) at most 80 rows name the same one
- gates: float32 [2048, 8], P('ep'), may hold values from 0.05 to 0.5
- pairing: int32 [1536], P('ep'), may hold values from 0 to 31
- w_gate: bfloat16 [16, 4096, 768], P('ep', 'rep'), may hold values from -0.09375 to 0.09375
- w_up: bfloat16 [16, 4096, 768], P('ep', 'rep'), may hold values from -0.09375 to 0.09375
- w_down: bfloat16 [16, 768, 4096], P('ep', None, 'rep'), may hold values from -0.21875 to 0.21875
Outputs:
- mixed: bfloat16 [2048, 4096], P('ep', 'rep')
- grad_gate: bfloat16 [16, 4096, 768], P('ep', 'rep')
- grad_up: bfloat16 [16, 4096, 768], P('ep', 'rep')
- grad_down: bfloat16 [16, 768, 4096], P('ep', None, 'rep')
The draws below stay inside these ranges and needn't reach their ends.
Inputs may be any that keep to these rules, and one draw needn't show every extreme that they name: `routes`: each row names 8 different experts. In each owner's block of 128 rows no expert is named by more than 80 rows, a bound that some block reaches. A token row's pairing counts from the first context row of its own block.
All inputs are finite; a program needn't handle non-finite values.
Results may differ from the reference program's by a relative error of at most 0.01.
Values may be sent and summed in bfloat16 or wider, within the bound.
A program may use at most 128 MiB of HBM per device.

```python
import math
import jax
import jax.numpy as jnp
import numpy as np
from jax import lax

D = 4096
HIDDEN_SIZE = 768
TOP = 8
TOK_DEV = 96
CTX_DEV = 32
ROW_DEV = 128
EXPERTS = 16
CAP = 80
SLOTS = 1280
ROWS = 2048
TOKENS = 1536
N_EP = 16


def plant(drawn, stream_key, smallest, top_value):
    spot = [jax.random.randint(jax.random.fold_in(stream_key, axis), (), 0, length) for axis, length in enumerate(drawn.shape)]
    longest = drawn.shape.index(max(drawn.shape))
    beside = spot[:longest] + [(spot[longest] + 1) % drawn.shape[longest]] + spot[longest + 1:]
    return drawn.at[tuple(spot)].set(smallest).at[tuple(beside)].set(top_value)


def block_scale(rng, extent, split, least, high):
    def one(axis_at, parts):
        heights = jax.random.uniform(jax.random.fold_in(jax.random.fold_in(rng, 6), axis_at), (parts,), jnp.float32, least / len(split), high / len(split))
        return jnp.repeat(jnp.exp(heights), extent[axis_at] // parts).reshape((-1,) + (1,) * (len(extent) - axis_at - 1))

    level = one(*split[0])
    for cut in split[1:]:
        level = level * one(*cut)
    return level


def deal_out(own_key, own, number, rows, number_of, top, bound, slope):
    sequence = jax.random.permutation(own_key, number_of)
    crowded, common = shares(number_of, rows * top, bound, slope, True), shares(number_of, rows * top, bound, slope, False)
    places = jnp.arange(number_of)

    def named(sizes, rotation):
        used = int((sizes > 0).sum())
        fixed = max(1, used // 4)
        shifted = fixed + (places - fixed + rotation * (used - fixed)) % max(1, number_of - fixed)
        return jnp.zeros((number_of,), jnp.int32).at[sequence[jnp.where(places < fixed, places, shifted)]].set(jnp.asarray(sizes, jnp.int32))

    sizes = jnp.where(number % 4 == 0, named(crowded, number // 4), named(common, number - number // 4 - 1))
    mixed = jax.random.permutation(jax.random.fold_in(own, 3), number_of)
    source_of, sink = mixed[0:number_of // 2 * 2:2], mixed[1:number_of // 2 * 2:2]
    slack = jnp.minimum(sizes[source_of] - 1, bound - sizes[sink]) // 2
    slack = jnp.where((source_of == sequence[0]) | (sink == sequence[0]) | (sizes[sink] == 0), 0, jnp.maximum(slack, 0))
    shifted = jax.random.randint(jax.random.fold_in(own, 4), (number_of // 2,), 0, 1 << 20) % (slack + 1)
    sizes = sizes.at[source_of].add(-shifted).at[sink].add(shifted)
    members = jnp.searchsorted(jnp.cumsum(sizes), jnp.arange(rows * top), side="right").astype(jnp.int32)
    grid = members.reshape(top, rows).T
    grid = grid[jax.random.permutation(jax.random.fold_in(own, 1), rows)]
    rotation = jax.random.randint(jax.random.fold_in(own, 2), (rows, 1), 0, top)
    return jnp.take_along_axis(grid, (jnp.arange(top)[None, :] + rotation) % top, axis=1)


def shares(number_of, total, bound, skew, full):
    weights = [(1 << 20) // math.isqrt(standing ** skew) + 1 for standing in range(1, number_of + 1)]
    largest = bound if full else min(bound, max(-(-total // number_of), total * weights[0] // sum(weights)))
    least = 1 if total - largest >= number_of - 1 else 0
    given, rest = [largest] + [least] * (number_of - 1), total - largest - least * (number_of - 1)
    while rest > 0:
        movable = [i for i in range(1, number_of) if given[i] < largest] or [i for i in range(1, number_of) if given[i] < bound]
        whole, remaining = sum([weights[i] for i in movable]), rest
        for i in movable:
            extra = min(bound - given[i], max(1, remaining * weights[i] // whole), rest)
            given[i] = given[i] + extra
            rest = rest - extra
    return np.array(given)


def gaussian(rng, shape, spread, limit, pieces=(), kind=jnp.bfloat16):
    result = spread * jax.random.normal(rng, shape, jnp.float32)
    if pieces:
        result = result * block_scale(rng, shape, pieces, -0.22, 0.18)
    return jnp.clip(result, -limit, limit).astype(kind)


def setup_inputs(seed: int = 0) -> dict:
    keys = jax.random.split(jax.random.key(seed), 8)
    signal = gaussian(keys[0], (ROWS, D), 1.0, 6.0, ((0, 16), (1, 2)))
    routes_keys = jax.random.split(jax.random.fold_in(keys[1], 1), ROWS // ROW_DEV)
    routes_turns = jax.random.permutation(jax.random.fold_in(keys[1], 3), ROWS // ROW_DEV)
    routes = jax.vmap(lambda own, number: deal_out(jax.random.fold_in(keys[1], 2), own, number, ROW_DEV, EXPERTS, TOP, CAP, 1))(routes_keys, routes_turns).reshape((ROWS, TOP))
    gates = jnp.clip(jnp.exp(math.log(0.5) - 2.3025851 * jax.random.uniform(keys[2], (ROWS, TOP), jnp.float32) ** block_scale(keys[2], (ROWS, TOP), ((0, 16),), -0.2, 0.2)), 0.05, 0.5)
    pairing = plant(jax.random.randint(keys[3], (TOKENS,), 0, CTX_DEV), jax.random.fold_in(keys[3], 1), 0, CTX_DEV - 1).astype(jnp.int32)
    w_gate = gaussian(keys[4], (EXPERTS, D, HIDDEN_SIZE), D ** -0.5, 0.09375, ((0, 16), (1, 2)))
    w_up = gaussian(keys[5], (EXPERTS, D, HIDDEN_SIZE), D ** -0.5, 0.09375, ((0, 16), (1, 2)))
    w_down = gaussian(keys[6], (EXPERTS, HIDDEN_SIZE, D), HIDDEN_SIZE ** -0.5, 0.21875, ((0, 16), (2, 2)))
    return dict(signal=signal, routes=routes, gates=gates, pairing=pairing, w_gate=w_gate, w_up=w_up, w_down=w_down)


epsilon = 1e-06

def route_slots(block_routes, capacity, experts):
    flat = block_routes.reshape(-1).astype(jnp.int32)
    onehot = (flat[:, None] == jnp.arange(experts, dtype=jnp.int32)[None, :]).astype(jnp.int32)
    position = lax.optimization_barrier(jnp.sum(jnp.cumsum(onehot, axis=0) * onehot, axis=1)) - 1
    return (flat, position.astype(jnp.int32))

def swish(gate, upper):
    return gate * jax.nn.sigmoid(gate) * upper

def row_gradient(combined, pair_block):
    squares = lax.optimization_barrier(jnp.sum(combined * combined, axis=1))
    scale = lax.rsqrt(squares / D + epsilon)
    normed = combined * scale[:, None]
    pair_table = (pair_block[:, None] == jnp.arange(CTX_DEV, dtype=jnp.int32)[None, :]).astype(jnp.float32)
    targets = jnp.dot(pair_table, normed[TOK_DEV:], precision=lax.Precision.HIGHEST)
    diff = normed[:TOK_DEV] - targets
    back = jnp.dot(pair_table.T, diff, precision=lax.Precision.HIGHEST)
    grad_normed = jnp.concatenate([diff, -back], axis=0) / TOK_DEV
    dots = lax.optimization_barrier(jnp.sum(grad_normed * normed, axis=1))
    return scale[:, None] * (grad_normed - normed * (dots / D)[:, None])

def reference(signal, routes, gates, pairing, w_gate, w_up, w_down):
    block_routes = routes.reshape(N_EP, ROW_DEV * TOP)
    experts_of, positions = jax.vmap(lambda blk: route_slots(blk, CAP, EXPERTS))(block_routes)
    block_index = jnp.arange(N_EP, dtype=jnp.int32)[:, None]
    global_slot = experts_of * SLOTS + block_index * CAP + positions
    row_index = block_index * ROW_DEV + (jnp.arange(ROW_DEV * TOP, dtype=jnp.int32) // TOP)[None, :]
    slot_row = jnp.full((EXPERTS * SLOTS,), ROWS, jnp.int32)
    slot_row = slot_row.at[global_slot.reshape(-1)].set(row_index.reshape(-1)).reshape(EXPERTS, SLOTS)
    padded = jnp.concatenate([signal, jnp.zeros((1, D), jnp.bfloat16)], axis=0)

    def expert_forward(inputs):
        rows_of, gate_weight, up_weight, down_weight = inputs
        arrived = padded[rows_of]
        gate = jnp.dot(arrived, gate_weight, preferred_element_type=jnp.float32)
        upper = jnp.dot(arrived, up_weight, preferred_element_type=jnp.float32)
        hidden = swish(gate, upper).astype(jnp.bfloat16)
        return jnp.dot(hidden, down_weight, preferred_element_type=jnp.float32).astype(jnp.bfloat16)
    outputs = lax.map(expert_forward, (slot_row, w_gate, w_up, w_down)).reshape(EXPERTS * SLOTS, D)

    def block_step(inputs):
        slot_block, gate_block, pair_block = inputs
        picked = outputs[slot_block].astype(jnp.float32).reshape(ROW_DEV, TOP, D)
        combined = lax.optimization_barrier(jnp.sum(picked * gate_block[:, :, None], axis=1))
        grad_rows = row_gradient(combined, pair_block)
        route_grad = (grad_rows[:, None, :] * gate_block[:, :, None]).astype(jnp.bfloat16)
        return (combined, route_grad.reshape(ROW_DEV * TOP, D))
    combined, route_grads = lax.map(block_step, (global_slot, gates.reshape(N_EP, ROW_DEV, TOP), pairing.reshape(N_EP, TOK_DEV)))
    grad_slots = jnp.zeros((EXPERTS * SLOTS, D), jnp.bfloat16)
    grad_slots = grad_slots.at[global_slot.reshape(-1)].set(route_grads.reshape(-1, D)).reshape(EXPERTS, SLOTS, D)

    def expert_backward(inputs):
        rows_of, grad_out, gate_weight, up_weight, down_weight = inputs
        arrived = padded[rows_of]
        gate = jnp.dot(arrived, gate_weight, preferred_element_type=jnp.float32)
        upper = jnp.dot(arrived, up_weight, preferred_element_type=jnp.float32)
        hidden = swish(gate, upper).astype(jnp.bfloat16)
        grad_down = jnp.dot(hidden.T, grad_out, preferred_element_type=jnp.float32)
        grad_hidden = jnp.dot(grad_out, down_weight.T, preferred_element_type=jnp.float32)
        sigma = jax.nn.sigmoid(gate)
        grad_gate_pre = (grad_hidden * upper * sigma * (1.0 + gate * (1.0 - sigma))).astype(jnp.bfloat16)
        grad_up_pre = (grad_hidden * gate * sigma).astype(jnp.bfloat16)
        grad_gate = jnp.dot(arrived.T, grad_gate_pre, preferred_element_type=jnp.float32)
        grad_upper = jnp.dot(arrived.T, grad_up_pre, preferred_element_type=jnp.float32)
        return (grad_gate.astype(jnp.bfloat16), grad_upper.astype(jnp.bfloat16), grad_down.astype(jnp.bfloat16))
    grad_gate, grad_upper, grad_down = lax.map(expert_backward, (slot_row, grad_slots, w_gate, w_up, w_down))
    mixed = combined.reshape(ROWS, D).astype(jnp.bfloat16)
    return (mixed, grad_gate, grad_upper, grad_down)
```

```python
import jax
import jax.numpy as jnp
from jax import lax
from jax.sharding import PartitionSpec as P

D = 4096
TOP = 8
EPSILON = 1e-06
BF = jnp.bfloat16
F32 = jnp.float32


def mm(a, b, ca=1, cb=0):
    return lax.dot_general(a, b, (((ca,), (cb,)), ((), ())), preferred_element_type=F32)


def blocks_mm(a, b, ca, cb):
    return lax.dot_general(a, b, (((ca,), (cb,)), ((0,), (0,))), preferred_element_type=F32)


def swap(value):
    return lax.ppermute(value, "rep", [(0, 1), (1, 0)])


def both_halves(own, other, rank):
    return jnp.where(
        rank == 0, jnp.concatenate([own, other], 0), jnp.concatenate([other, own], 0)
    )


def half_sum(value, rank):
    half = value.shape[0] // 2
    theirs = lax.dynamic_slice_in_dim(value, (1 - rank) * half, half, 0)
    mine = lax.dynamic_slice_in_dim(value, rank * half, half, 0)
    return mine.astype(F32) + swap(theirs).astype(F32)


def local(signal, routes, gates, pairing, w_gate, w_up, w_down):
    experts = lax.axis_size("ep")
    shards = lax.axis_size("rep")
    rank = lax.axis_index("rep")
    row_count, width = signal.shape
    tokens = pairing.shape[0]
    contexts = row_count - tokens
    capacity = min(row_count, row_count * TOP * 5 // (4 * experts))
    w_gate, w_up, w_down = w_gate[0], w_up[0], w_down[0]
    hidden_width = w_gate.shape[1]

    rows_all = lax.all_gather(signal, "ep", axis=0, tiled=True)

    expert_ids = jnp.arange(experts, dtype=jnp.int32)
    table = jnp.sum(
        jnp.where(routes[:, None, :] == expert_ids[None, :, None], gates[:, None, :], 0.0), axis=2
    )
    weight = lax.all_to_all(table.T, "ep", split_axis=0, concat_axis=0, tiled=True)
    chosen = weight > 0.0
    before = jnp.arange(row_count)[:, None] < jnp.arange(row_count)[None, :]
    position = jnp.dot(
        chosen.astype(BF), before.astype(BF), preferred_element_type=F32
    ).astype(jnp.int32)
    pick = (
        (position[:, None, :] == jnp.arange(capacity, dtype=jnp.int32)[None, :, None])
        & chosen[:, None, :]
    ).astype(BF)
    row_weight = weight.reshape(experts * row_count, 1)

    arrived = (
        blocks_mm(pick, rows_all.reshape(experts, row_count, width), 2, 1)
        .astype(BF)
        .reshape(experts * capacity, width)
    )
    gate_part = mm(arrived, w_gate)
    up_part = mm(arrived, w_up)
    if shards == 2:
        gate_own = half_sum(gate_part.astype(BF), rank)
        up_own = half_sum(up_part.astype(BF), rank)
        hidden_own = (gate_own * jax.nn.sigmoid(gate_own) * up_own).astype(BF)
        hidden = both_halves(hidden_own, swap(hidden_own), rank)
        gate_own, up_own = gate_own.astype(BF), up_own.astype(BF)
        gate_all = both_halves(gate_own, swap(gate_own), rank)
        up_all = both_halves(up_own, swap(up_own), rank)
    else:
        gate_all, up_all = lax.psum((gate_part, up_part), "rep")
        hidden = (gate_all * jax.nn.sigmoid(gate_all) * up_all).astype(BF)

    spread = (
        blocks_mm(pick, hidden.reshape(experts, capacity, hidden_width), 1, 1)
        .astype(BF)
        .reshape(experts * row_count, hidden_width)
    )
    returned = (mm(spread, w_down) * row_weight).astype(BF)
    mixed = lax.psum_scatter(returned, "ep", scatter_dimension=0, tiled=True)
    combined = mixed.astype(F32)

    pair = (pairing[:, None] == jnp.arange(contexts, dtype=jnp.int32)[None, :]).astype(F32)

    def pick_context(value):
        return jnp.dot(pair, value, precision=lax.Precision.HIGHEST)

    def per_context(value):
        return jnp.dot(pair.T, value, precision=lax.Precision.HIGHEST)

    matched = pick_context(combined[tokens:])
    sums = lax.psum(
        jnp.concatenate(
            [jnp.sum(combined * combined, axis=1), jnp.sum(combined[:tokens] * matched, axis=1)]
        ),
        "rep",
    )
    squares, cross = sums[:row_count], sums[row_count:]
    scale = lax.rsqrt(squares / D + EPSILON)
    token_scale, context_scale = scale[:tokens], scale[tokens:]
    paired_scale = jnp.sum(pair * context_scale[None, :], axis=1)
    norm_squares = squares * scale * scale
    cross = cross * token_scale * paired_scale
    paired_squares = jnp.sum(pair * norm_squares[None, tokens:], axis=1)
    dots = jnp.concatenate(
        [
            norm_squares[:tokens] - cross,
            jnp.sum(pair * (paired_squares - cross)[:, None], axis=0),
        ]
    ) / tokens
    normed = combined * scale[:, None]
    diff = normed[:tokens] - matched * paired_scale[:, None]
    grad_normed = jnp.concatenate([diff, -per_context(diff)], axis=0) / tokens
    grad_rows = (scale[:, None] * (grad_normed - normed * (dots / D)[:, None])).astype(BF)

    grads_all = lax.all_gather(grad_rows, "ep", axis=0, tiled=True)
    grad_hidden_rows = (mm(grads_all, w_down, 1, 1) * row_weight).astype(BF)
    grad_hidden_part = blocks_mm(
        pick, grad_hidden_rows.reshape(experts, row_count, hidden_width), 2, 1
    ).reshape(experts * capacity, hidden_width)
    if shards == 2:
        sent = grad_hidden_part.astype(BF)
        grad_hidden = sent.astype(F32) + swap(sent).astype(F32)
    else:
        grad_hidden = lax.psum(grad_hidden_part, "rep")
    weighted = (spread.astype(F32) * row_weight).astype(BF)
    grad_down = mm(weighted, grads_all, 0, 0).astype(BF)

    gate_all, up_all = gate_all.astype(F32), up_all.astype(F32)
    sigma = jax.nn.sigmoid(gate_all)
    grad_gate_pre = (grad_hidden * up_all * sigma * (1.0 + gate_all * (1.0 - sigma))).astype(BF)
    grad_up_pre = (grad_hidden * gate_all * sigma).astype(BF)
    grad_gate = mm(arrived, grad_gate_pre, 0, 0).astype(BF)
    grad_up = mm(arrived, grad_up_pre, 0, 0).astype(BF)
    return (mixed, grad_gate[None], grad_up[None], grad_down[None])


def solution(mesh):
    return jax.shard_map(
        local,
        mesh=mesh,
        in_specs=(
            P("ep", "rep"),
            P("ep", None),
            P("ep", None),
            P("ep"),
            P("ep", "rep", None),
            P("ep", "rep", None),
            P("ep", None, "rep"),
        ),
        out_specs=(
            P("ep", "rep"),
            P("ep", "rep", None),
            P("ep", "rep", None),
            P("ep", None, "rep"),
        ),
        check_vma=False,
    )
```

```python
import jax
import jax.numpy as jnp
from jax import lax
from jax.sharding import PartitionSpec as P

D = 4096
TOP = 8
EPSILON = 1e-06
BF = jnp.bfloat16
F32 = jnp.float32


def mm(a, b, ca=1, cb=0):
    return lax.dot_general(a, b, (((ca,), (cb,)), ((), ())), preferred_element_type=F32)


def blocks_mm(a, b, ca, cb):
    return lax.dot_general(a, b, (((ca,), (cb,)), ((0,), (0,))), preferred_element_type=F32)


def swap(value):
    return lax.ppermute(value, "rep", [(0, 1), (1, 0)])


def both_halves(own, other, rank):
    return jnp.where(
        rank == 0, jnp.concatenate([own, other], 0), jnp.concatenate([other, own], 0)
    )


def half_sum(value, rank):
    half = value.shape[0] // 2
    theirs = lax.dynamic_slice_in_dim(value, (1 - rank) * half, half, 0)
    mine = lax.dynamic_slice_in_dim(value, rank * half, half, 0)
    return mine.astype(F32) + swap(theirs).astype(F32)


def row_gradient(combined, pairing):
    row_count, tokens = combined.shape[0], pairing.shape[0]
    contexts = row_count - tokens
    pair = (pairing[:, None] == jnp.arange(contexts, dtype=jnp.int32)[None, :]).astype(F32)

    def pick_context(value):
        return jnp.dot(pair, value, precision=lax.Precision.HIGHEST)

    def per_context(value):
        return jnp.dot(pair.T, value, precision=lax.Precision.HIGHEST)

    matched = pick_context(combined[tokens:])
    sums = lax.psum(
        jnp.concatenate(
            [jnp.sum(combined * combined, axis=1), jnp.sum(combined[:tokens] * matched, axis=1)]
        ),
        "rep",
    )
    squares, cross = sums[:row_count], sums[row_count:]
    scale = lax.rsqrt(squares / D + EPSILON)
    token_scale, context_scale = scale[:tokens], scale[tokens:]
    paired_scale = jnp.sum(pair * context_scale[None, :], axis=1)
    norm_squares = squares * scale * scale
    cross = cross * token_scale * paired_scale
    paired_squares = jnp.sum(pair * norm_squares[None, tokens:], axis=1)
    dots = jnp.concatenate(
        [
            norm_squares[:tokens] - cross,
            jnp.sum(pair * (paired_squares - cross)[:, None], axis=0),
        ]
    ) / tokens
    normed = combined * scale[:, None]
    diff = normed[:tokens] - matched * paired_scale[:, None]
    grad_normed = jnp.concatenate([diff, -per_context(diff)], axis=0) / tokens
    grad_rows = (scale[:, None] * (grad_normed - normed * (dots / D)[:, None])).astype(BF)
    return grad_rows


def gate_table(routes, gates, experts):
    expert_ids = jnp.arange(experts, dtype=jnp.int32)
    table = jnp.sum(
        jnp.where(routes[:, None, :] == expert_ids[None, :, None], gates[:, None, :], 0.0), axis=2
    )
    return lax.all_to_all(table.T, "ep", split_axis=0, concat_axis=0, tiled=True)


def slot_picks(weight, capacity):
    row_count = weight.shape[1]
    chosen = weight > 0.0
    before = jnp.arange(row_count)[:, None] < jnp.arange(row_count)[None, :]
    position = jnp.dot(
        chosen.astype(BF), before.astype(BF), preferred_element_type=F32
    ).astype(jnp.int32)
    return (
        (position[:, None, :] == jnp.arange(capacity, dtype=jnp.int32)[None, :, None])
        & chosen[:, None, :]
    ).astype(BF)


def local_general(signal, routes, gates, pairing, w_gate, w_up, w_down):
    experts = lax.axis_size("ep")
    row_count, width = signal.shape
    capacity = min(row_count, row_count * TOP * 5 // (4 * experts))
    w_gate, w_up, w_down = w_gate[0], w_up[0], w_down[0]
    hidden_width = w_gate.shape[1]

    rows_all = lax.all_gather(signal, "ep", axis=0, tiled=True)

    weight = gate_table(routes, gates, experts)
    pick = slot_picks(weight, capacity)
    row_weight = weight.reshape(experts * row_count, 1)

    arrived = (
        blocks_mm(pick, rows_all.reshape(experts, row_count, width), 2, 1)
        .astype(BF)
        .reshape(experts * capacity, width)
    )
    gate_part = mm(arrived, w_gate)
    up_part = mm(arrived, w_up)
    gate_all, up_all = lax.psum((gate_part, up_part), "rep")
    hidden = (gate_all * jax.nn.sigmoid(gate_all) * up_all).astype(BF)

    spread = (
        blocks_mm(pick, hidden.reshape(experts, capacity, hidden_width), 1, 1)
        .astype(BF)
        .reshape(experts * row_count, hidden_width)
    )
    returned = (mm(spread, w_down) * row_weight).astype(BF)
    mixed = lax.psum_scatter(returned, "ep", scatter_dimension=0, tiled=True)
    combined = mixed.astype(F32)

    grad_rows = row_gradient(combined, pairing)
    grads_all = lax.all_gather(grad_rows, "ep", axis=0, tiled=True)
    grad_hidden_rows = (mm(grads_all, w_down, 1, 1) * row_weight).astype(BF)
    grad_hidden_part = blocks_mm(
        pick, grad_hidden_rows.reshape(experts, row_count, hidden_width), 2, 1
    ).reshape(experts * capacity, hidden_width)
    grad_hidden = lax.psum(grad_hidden_part, "rep")
    weighted = (spread.astype(F32) * row_weight).astype(BF)
    grad_down = mm(weighted, grads_all, 0, 0).astype(BF)

    gate_all, up_all = gate_all.astype(F32), up_all.astype(F32)
    sigma = jax.nn.sigmoid(gate_all)
    grad_gate_pre = (grad_hidden * up_all * sigma * (1.0 + gate_all * (1.0 - sigma))).astype(BF)
    grad_up_pre = (grad_hidden * gate_all * sigma).astype(BF)
    grad_gate = mm(arrived, grad_gate_pre, 0, 0).astype(BF)
    grad_up = mm(arrived, grad_up_pre, 0, 0).astype(BF)
    return (mixed, grad_gate[None], grad_up[None], grad_down[None])


Z = 4


def across(value, bit):
    return lax.ppermute(value, "ep", [(i, i ^ bit) for i in range(4 * Z)])


def across_x(value, low, high):
    return lax.ppermute(
        value, "ep", [(z * 4 + i, z * 4 + (i ^ 2)) for z in range(low, high) for i in range(4)]
    )


def along_z(value, low, high, step):
    return lax.ppermute(
        value,
        "ep",
        [(z * 4 + i, (z + step) * 4 + i) for z in range(low, high) for i in range(4)],
    )


def gather_groups(value):
    up1 = along_z(value, 0, 3, 1)
    down1 = along_z(value, 1, 4, -1)
    side0 = across_x(value, 0, 4)
    up2 = along_z(up1, 1, 3, 1)
    down2 = along_z(down1, 1, 3, -1)
    side_up1 = across_x(up1, 1, 4)
    side_down1 = across_x(down1, 0, 3)
    up3 = along_z(up2, 2, 3, 1)
    down3 = along_z(down2, 1, 2, -1)
    side_up2 = across_x(up2, 2, 4)
    side_down2 = across_x(down2, 0, 2)
    side_up3 = across_x(up3, 3, 4)
    side_down3 = across_x(down3, 0, 1)
    pairs = [
        (value, side0),
        (up1 + down3, side_up1 + side_down3),
        (up2 + down2, side_up2 + side_down2),
        (up3 + down1, side_up3 + side_down1),
    ]
    groups = []
    for own, side in pairs:
        mine = jnp.concatenate([own, side], 0)
        other = across(mine, 1)
        groups.append(jnp.concatenate([mine, other], 0))
    return groups


def scatter_sum(value):
    def add(a, b):
        return (a.astype(F32) + b.astype(F32)).astype(BF)

    value = add(value[:, 0], across(value[:, 1], 1))
    value = add(value[:, 0], across(value[:, 1], 2))
    up = along_z(value[1], 0, 1, 1)
    down = along_z(value[3], 3, 4, -1)
    up = along_z(add(value[2], up), 0, 2, 1)
    down = along_z(add(value[2], down), 2, 4, -1)
    up = along_z(add(value[3], up), 0, 3, 1)
    down = along_z(add(value[1], down), 1, 4, -1)
    return value[0].astype(F32) + up.astype(F32) + down.astype(F32)


ORDER = (0, 2, 1, 3)
CHUNKS = 4


def local(signal, routes, gates, pairing, w_gate, w_up, w_down):
    experts = lax.axis_size("ep")
    rank = lax.axis_index("rep")
    me = lax.axis_index("ep")
    row_count, width = signal.shape
    capacity = min(row_count, row_count * TOP * 5 // (4 * experts))
    w_gate, w_up, w_down = w_gate[0], w_up[0], w_down[0]
    hidden_width = w_gate.shape[1]
    w_both = jnp.concatenate([w_gate, w_up], 1)

    row_groups = gather_groups(signal)
    weight = gate_table(routes, gates, experts)
    place = jnp.arange(experts, dtype=jnp.int32)
    owner = ((me // 4 - place // 4 + Z) % Z) * 4 + (me % 4) ^ (place % 2 * 2 + place // 2 % 2)
    weight = jnp.take(weight, owner, axis=0)
    pick = slot_picks(weight, capacity).reshape(Z, 4, capacity, row_count)
    row_weight = weight.reshape(Z, 4 * row_count, 1)

    arrived, hidden, gate_up, spread = [None] * Z, [None] * Z, [None] * Z, [None] * Z
    for k in ORDER:
        rows = row_groups[k].reshape(4, row_count, width)
        arrived[k] = blocks_mm(pick[k], rows, 2, 1).astype(BF).reshape(4 * capacity, width)
        own = half_sum(mm(arrived[k], w_both).astype(BF), rank)
        gate, up = own[:, :hidden_width], own[:, hidden_width:]
        hidden_own = (gate * jax.nn.sigmoid(gate) * up).astype(BF)
        gate_up[k] = own.astype(BF)
        hidden[k] = both_halves(hidden_own, swap(hidden_own), rank)
        spread[k] = (
            blocks_mm(pick[k], hidden[k].reshape(4, capacity, hidden_width), 1, 1)
            .astype(BF)
            .reshape(4 * row_count, hidden_width)
        )
    spread = jnp.concatenate(spread, 0)
    all_weight = weight.reshape(experts * row_count, 1)

    part = width // CHUNKS
    combined = []
    for c in range(CHUNKS):
        returned = (mm(spread, w_down[:, c * part : (c + 1) * part]) * all_weight).astype(BF)
        combined.append(scatter_sum(returned.reshape(Z, 2, 2, row_count, part)))
    combined = jnp.concatenate(combined, 1)
    others = [swap(value) for value in gate_up]
    combined, others = lax.optimization_barrier((combined, others))
    mixed = combined.astype(BF)
    grad_rows = row_gradient(combined, pairing)

    grad_groups = gather_groups(grad_rows)
    gate_pre, up_pre = [None] * Z, [None] * Z
    for k in ORDER:
        rows = (mm(grad_groups[k], w_down, 1, 1) * row_weight[k]).astype(BF)
        sent = (
            blocks_mm(pick[k], rows.reshape(4, row_count, hidden_width), 2, 1)
            .reshape(4 * capacity, hidden_width)
            .astype(BF)
        )
        grad_hidden = sent.astype(F32) + swap(sent).astype(F32)
        both = both_halves(gate_up[k], others[k], rank).astype(F32)
        gate, up = both[:, :hidden_width], both[:, hidden_width:]
        sigma = jax.nn.sigmoid(gate)
        gate_pre[k] = (grad_hidden * up * sigma * (1.0 + gate * (1.0 - sigma))).astype(BF)
        up_pre[k] = (grad_hidden * gate * sigma).astype(BF)
    weighted = (spread.astype(F32) * all_weight).astype(BF)
    grad_down = mm(weighted, jnp.concatenate(grad_groups, 0), 0, 0).astype(BF)
    arrived = jnp.concatenate(arrived, 0)
    grad_gate = mm(arrived, jnp.concatenate(gate_pre, 0), 0, 0).astype(BF)
    grad_up = mm(arrived, jnp.concatenate(up_pre, 0), 0, 0).astype(BF)
    return (mixed, grad_gate[None], grad_up[None], grad_down[None])


def solution(mesh):
    blocked = mesh.shape["ep"] == 4 * Z and mesh.shape["rep"] == 2
    return jax.shard_map(
        local if blocked else local_general,
        mesh=mesh,
        in_specs=(
            P("ep", "rep"),
            P("ep", None),
            P("ep", None),
            P("ep"),
            P("ep", "rep", None),
            P("ep", "rep", None),
            P("ep", None, "rep"),
        ),
        out_specs=(
            P("ep", "rep"),
            P("ep", "rep", None),
            P("ep", "rep", None),
            P("ep", None, "rep"),
        ),
        check_vma=False,
    )
```

```python
import jax
import jax.numpy as jnp
from jax import lax
from jax.sharding import PartitionSpec as P

D = 4096
TOP = 8
EPSILON = 1e-06
BF = jnp.bfloat16
F32 = jnp.float32


def mm(a, b, ca=1, cb=0):
    return lax.dot_general(a, b, (((ca,), (cb,)), ((), ())), preferred_element_type=F32)


def blocks_mm(a, b, ca, cb):
    return lax.dot_general(a, b, (((ca,), (cb,)), ((0,), (0,))), preferred_element_type=F32)


def swap(value):
    return lax.ppermute(value, "rep", [(0, 1), (1, 0)])


def both_halves(own, other, rank):
    return jnp.where(
        rank == 0, jnp.concatenate([own, other], 0), jnp.concatenate([other, own], 0)
    )


def half_sum(value, rank):
    half = value.shape[0] // 2
    theirs = lax.dynamic_slice_in_dim(value, (1 - rank) * half, half, 0)
    mine = lax.dynamic_slice_in_dim(value, rank * half, half, 0)
    return mine.astype(F32) + swap(theirs).astype(F32)


def row_gradient(combined, pairing):
    row_count, tokens = combined.shape[0], pairing.shape[0]
    contexts = row_count - tokens
    pair = (pairing[:, None] == jnp.arange(contexts, dtype=jnp.int32)[None, :]).astype(F32)

    def pick_context(value):
        return jnp.dot(pair, value, precision=lax.Precision.HIGHEST)

    def per_context(value):
        return jnp.dot(pair.T, value, precision=lax.Precision.HIGHEST)

    matched = pick_context(combined[tokens:])
    sums = lax.psum(
        jnp.concatenate(
            [jnp.sum(combined * combined, axis=1), jnp.sum(combined[:tokens] * matched, axis=1)]
        ),
        "rep",
    )
    squares, cross = sums[:row_count], sums[row_count:]
    scale = lax.rsqrt(squares / D + EPSILON)
    token_scale, context_scale = scale[:tokens], scale[tokens:]
    paired_scale = jnp.sum(pair * context_scale[None, :], axis=1)
    norm_squares = squares * scale * scale
    cross = cross * token_scale * paired_scale
    paired_squares = jnp.sum(pair * norm_squares[None, tokens:], axis=1)
    dots = jnp.concatenate(
        [
            norm_squares[:tokens] - cross,
            jnp.sum(pair * (paired_squares - cross)[:, None], axis=0),
        ]
    ) / tokens
    normed = combined * scale[:, None]
    diff = normed[:tokens] - matched * paired_scale[:, None]
    grad_normed = jnp.concatenate([diff, -per_context(diff)], axis=0) / tokens
    grad_rows = (scale[:, None] * (grad_normed - normed * (dots / D)[:, None])).astype(BF)
    return grad_rows


def gate_table(routes, gates, experts):
    expert_ids = jnp.arange(experts, dtype=jnp.int32)
    table = jnp.sum(
        jnp.where(routes[:, None, :] == expert_ids[None, :, None], gates[:, None, :], 0.0), axis=2
    )
    return lax.all_to_all(table.T, "ep", split_axis=0, concat_axis=0, tiled=True)


def slot_picks(weight, capacity):
    row_count = weight.shape[1]
    chosen = weight > 0.0
    before = jnp.arange(row_count)[:, None] < jnp.arange(row_count)[None, :]
    position = jnp.dot(
        chosen.astype(BF), before.astype(BF), preferred_element_type=F32
    ).astype(jnp.int32)
    return (
        (position[:, None, :] == jnp.arange(capacity, dtype=jnp.int32)[None, :, None])
        & chosen[:, None, :]
    ).astype(BF)


def local_general(signal, routes, gates, pairing, w_gate, w_up, w_down):
    experts = lax.axis_size("ep")
    row_count, width = signal.shape
    capacity = min(row_count, row_count * TOP * 5 // (4 * experts))
    w_gate, w_up, w_down = w_gate[0], w_up[0], w_down[0]
    hidden_width = w_gate.shape[1]

    rows_all = lax.all_gather(signal, "ep", axis=0, tiled=True)

    weight = gate_table(routes, gates, experts)
    pick = slot_picks(weight, capacity)
    row_weight = weight.reshape(experts * row_count, 1)

    arrived = (
        blocks_mm(pick, rows_all.reshape(experts, row_count, width), 2, 1)
        .astype(BF)
        .reshape(experts * capacity, width)
    )
    gate_part = mm(arrived, w_gate)
    up_part = mm(arrived, w_up)
    gate_all, up_all = lax.psum((gate_part, up_part), "rep")
    hidden = (gate_all * jax.nn.sigmoid(gate_all) * up_all).astype(BF)

    spread = (
        blocks_mm(pick, hidden.reshape(experts, capacity, hidden_width), 1, 1)
        .astype(BF)
        .reshape(experts * row_count, hidden_width)
    )
    returned = (mm(spread, w_down) * row_weight).astype(BF)
    mixed = lax.psum_scatter(returned, "ep", scatter_dimension=0, tiled=True)
    combined = mixed.astype(F32)

    grad_rows = row_gradient(combined, pairing)
    grads_all = lax.all_gather(grad_rows, "ep", axis=0, tiled=True)
    grad_hidden_rows = (mm(grads_all, w_down, 1, 1) * row_weight).astype(BF)
    grad_hidden_part = blocks_mm(
        pick, grad_hidden_rows.reshape(experts, row_count, hidden_width), 2, 1
    ).reshape(experts * capacity, hidden_width)
    grad_hidden = lax.psum(grad_hidden_part, "rep")
    weighted = (spread.astype(F32) * row_weight).astype(BF)
    grad_down = mm(weighted, grads_all, 0, 0).astype(BF)

    gate_all, up_all = gate_all.astype(F32), up_all.astype(F32)
    sigma = jax.nn.sigmoid(gate_all)
    grad_gate_pre = (grad_hidden * up_all * sigma * (1.0 + gate_all * (1.0 - sigma))).astype(BF)
    grad_up_pre = (grad_hidden * gate_all * sigma).astype(BF)
    grad_gate = mm(arrived, grad_gate_pre, 0, 0).astype(BF)
    grad_up = mm(arrived, grad_up_pre, 0, 0).astype(BF)
    return (mixed, grad_gate[None], grad_up[None], grad_down[None])


def across(value):
    count = lax.axis_size("ep")
    return lax.ppermute(value, "ep", [(i, i ^ 1) for i in range(count)])


def same_core():
    count = lax.axis_size("ep")
    return [list(range(core, count, 2)) for core in range(2)]


def gather_core(value):
    return lax.all_gather(value, "ep", axis=0, tiled=True, axis_index_groups=same_core())


def with_other_core(mine):
    half = mine.shape[0] // 2
    return [mine, across(mine[:half]), across(mine[half:])]


def local(signal, routes, gates, pairing, w_gate, w_up, w_down):
    experts = lax.axis_size("ep")
    rank = lax.axis_index("rep")
    core = lax.axis_index("ep") % 2
    row_count, width = signal.shape
    capacity = min(row_count, row_count * TOP * 5 // (4 * experts))
    w_gate, w_up, w_down = w_gate[0], w_up[0], w_down[0]
    hidden_width = w_gate.shape[1]
    half, quarter = experts // 2, experts // 4
    spans = ((0, half), (half, half + quarter), (half + quarter, experts))

    mine, w_down_other = lax.optimization_barrier((gather_core(signal), across(w_down)))
    row_groups = with_other_core(mine)
    w_down_pair = jnp.concatenate([w_down, w_down_other], 0)
    w_both = jnp.concatenate([w_gate, w_up], 1)
    weight = gate_table(routes, gates, experts).reshape(half, 2, row_count)
    weight = jnp.where(
        core == 0,
        jnp.concatenate([weight[:, 0], weight[:, 1]], 0),
        jnp.concatenate([weight[:, 1], weight[:, 0]], 0),
    )
    pick = slot_picks(weight, capacity)
    row_weight = weight.reshape(experts * row_count, 1)

    arrived, gate_up, weighted, handed = [], [], [], []
    for (low, high), rows in zip(spans, row_groups):
        count = high - low
        chosen = pick[low:high]
        arrived.append(
            blocks_mm(chosen, rows.reshape(count, row_count, width), 2, 1)
            .astype(BF)
            .reshape(count * capacity, width)
        )
        own = half_sum(mm(arrived[-1], w_both).astype(BF), rank)
        gate, up = own[:, :hidden_width], own[:, hidden_width:]
        hidden_own = (gate * jax.nn.sigmoid(gate) * up).astype(BF)
        gate_up.append(own.astype(BF))
        hidden = both_halves(hidden_own, swap(hidden_own), rank)
        spread = blocks_mm(chosen, hidden.reshape(count, capacity, hidden_width), 1, 1).reshape(
            count * row_count, hidden_width
        )
        weighted.append((spread * row_weight[low * row_count : high * row_count]).astype(BF))
        if low > 0:
            handed.append(across(weighted[-1]))

    inner = jnp.concatenate([weighted[0], jnp.concatenate(handed, 0)], 1)
    returned = mm(inner, w_down_pair).astype(BF)
    combined = lax.psum_scatter(
        returned, "ep", scatter_dimension=0, tiled=True, axis_index_groups=same_core()
    )
    others = [swap(value) for value in gate_up]
    combined, others = lax.optimization_barrier((combined, others))
    mixed = combined
    grad_rows = row_gradient(combined.astype(F32), pairing)

    grad_groups = with_other_core(gather_core(grad_rows))
    gate_pre, up_pre = [], []
    for (low, high), rows, own, other in zip(spans, grad_groups, gate_up, others):
        count = high - low
        product = (mm(rows, w_down, 1, 1) * row_weight[low * row_count : high * row_count]).astype(BF)
        sent = (
            blocks_mm(pick[low:high], product.reshape(count, row_count, hidden_width), 2, 1)
            .reshape(count * capacity, hidden_width)
            .astype(BF)
        )
        grad_hidden = sent.astype(F32) + swap(sent).astype(F32)
        both = both_halves(own, other, rank).astype(F32)
        gate, up = both[:, :hidden_width], both[:, hidden_width:]
        sigma = jax.nn.sigmoid(gate)
        gate_pre.append(
            (grad_hidden * up * sigma * (1.0 + gate * (1.0 - sigma))).astype(BF)
        )
        up_pre.append((grad_hidden * gate * sigma).astype(BF))
    grad_down = mm(
        jnp.concatenate(weighted, 0), jnp.concatenate(grad_groups, 0), 0, 0
    ).astype(BF)
    arrived = jnp.concatenate(arrived, 0)
    grad_gate = mm(arrived, jnp.concatenate(gate_pre, 0), 0, 0).astype(BF)
    grad_up = mm(arrived, jnp.concatenate(up_pre, 0), 0, 0).astype(BF)
    return (mixed, grad_gate[None], grad_up[None], grad_down[None])


def solution(mesh):
    blocked = mesh.shape["ep"] % 4 == 0 and mesh.shape["rep"] == 2
    return jax.shard_map(
        local if blocked else local_general,
        mesh=mesh,
        in_specs=(
            P("ep", "rep"),
            P("ep", None),
            P("ep", None),
            P("ep"),
            P("ep", "rep", None),
            P("ep", "rep", None),
            P("ep", None, "rep"),
        ),
        out_specs=(
            P("ep", "rep"),
            P("ep", "rep", None),
            P("ep", "rep", None),
            P("ep", None, "rep"),
        ),
        check_vma=False,
    )
```

```python
import jax
import jax.numpy as jnp
from jax import lax
from jax.sharding import PartitionSpec as P

D = 4096
TOP = 8
EPSILON = 1e-06
GROUPS = 4
BF = jnp.bfloat16
F32 = jnp.float32


def mm(a, b, ca=1, cb=0):
    return lax.dot_general(a, b, (((ca,), (cb,)), ((), ())), preferred_element_type=F32)


def blocks_mm(a, b, ca, cb):
    return lax.dot_general(a, b, (((ca,), (cb,)), ((0,), (0,))), preferred_element_type=F32)


def swap(value):
    return lax.ppermute(value, "rep", [(0, 1), (1, 0)])


def both_halves(own, other, rank):
    return jnp.where(
        rank == 0, jnp.concatenate([own, other], 0), jnp.concatenate([other, own], 0)
    )


def half_sum(value, rank):
    half = value.shape[0] // 2
    theirs = lax.dynamic_slice_in_dim(value, (1 - rank) * half, half, 0)
    mine = lax.dynamic_slice_in_dim(value, rank * half, half, 0)
    return mine.astype(F32) + swap(theirs).astype(F32)


def row_gradient(combined, pairing):
    row_count, tokens = combined.shape[0], pairing.shape[0]
    contexts = row_count - tokens
    pair = (pairing[:, None] == jnp.arange(contexts, dtype=jnp.int32)[None, :]).astype(F32)

    def pick_context(value):
        return jnp.dot(pair, value, precision=lax.Precision.HIGHEST)

    def per_context(value):
        return jnp.dot(pair.T, value, precision=lax.Precision.HIGHEST)

    matched = pick_context(combined[tokens:])
    sums = lax.psum(
        jnp.concatenate(
            [jnp.sum(combined * combined, axis=1), jnp.sum(combined[:tokens] * matched, axis=1)]
        ),
        "rep",
    )
    squares, cross = sums[:row_count], sums[row_count:]
    scale = lax.rsqrt(squares / D + EPSILON)
    token_scale, context_scale = scale[:tokens], scale[tokens:]
    paired_scale = jnp.sum(pair * context_scale[None, :], axis=1)
    norm_squares = squares * scale * scale
    cross = cross * token_scale * paired_scale
    paired_squares = jnp.sum(pair * norm_squares[None, tokens:], axis=1)
    dots = jnp.concatenate(
        [
            norm_squares[:tokens] - cross,
            jnp.sum(pair * (paired_squares - cross)[:, None], axis=0),
        ]
    ) / tokens
    normed = combined * scale[:, None]
    diff = normed[:tokens] - matched * paired_scale[:, None]
    grad_normed = jnp.concatenate([diff, -per_context(diff)], axis=0) / tokens
    grad_rows = (scale[:, None] * (grad_normed - normed * (dots / D)[:, None])).astype(BF)
    return grad_rows


def gate_table(routes, gates, experts):
    expert_ids = jnp.arange(experts, dtype=jnp.int32)
    table = jnp.sum(
        jnp.where(routes[:, None, :] == expert_ids[None, :, None], gates[:, None, :], 0.0), axis=2
    )
    return lax.all_to_all(table.T, "ep", split_axis=0, concat_axis=0, tiled=True)


def slot_picks(weight, capacity):
    row_count = weight.shape[1]
    chosen = weight > 0.0
    before = jnp.arange(row_count)[:, None] < jnp.arange(row_count)[None, :]
    position = jnp.dot(
        chosen.astype(BF), before.astype(BF), preferred_element_type=F32
    ).astype(jnp.int32)
    return (
        (position[:, None, :] == jnp.arange(capacity, dtype=jnp.int32)[None, :, None])
        & chosen[:, None, :]
    ).astype(BF)


def local_general(signal, routes, gates, pairing, w_gate, w_up, w_down):
    experts = lax.axis_size("ep")
    row_count, width = signal.shape
    capacity = min(row_count, row_count * TOP * 5 // (4 * experts))
    w_gate, w_up, w_down = w_gate[0], w_up[0], w_down[0]
    hidden_width = w_gate.shape[1]

    rows_all = lax.all_gather(signal, "ep", axis=0, tiled=True)

    weight = gate_table(routes, gates, experts)
    pick = slot_picks(weight, capacity)
    row_weight = weight.reshape(experts * row_count, 1)

    arrived = (
        blocks_mm(pick, rows_all.reshape(experts, row_count, width), 2, 1)
        .astype(BF)
        .reshape(experts * capacity, width)
    )
    gate_part = mm(arrived, w_gate)
    up_part = mm(arrived, w_up)
    gate_all, up_all = lax.psum((gate_part, up_part), "rep")
    hidden = (gate_all * jax.nn.sigmoid(gate_all) * up_all).astype(BF)

    spread = (
        blocks_mm(pick, hidden.reshape(experts, capacity, hidden_width), 1, 1)
        .astype(BF)
        .reshape(experts * row_count, hidden_width)
    )
    returned = (mm(spread, w_down) * row_weight).astype(BF)
    mixed = lax.psum_scatter(returned, "ep", scatter_dimension=0, tiled=True)
    combined = mixed.astype(F32)

    grad_rows = row_gradient(combined, pairing)
    grads_all = lax.all_gather(grad_rows, "ep", axis=0, tiled=True)
    grad_hidden_rows = (mm(grads_all, w_down, 1, 1) * row_weight).astype(BF)
    grad_hidden_part = blocks_mm(
        pick, grad_hidden_rows.reshape(experts, row_count, hidden_width), 2, 1
    ).reshape(experts * capacity, hidden_width)
    grad_hidden = lax.psum(grad_hidden_part, "rep")
    weighted = (spread.astype(F32) * row_weight).astype(BF)
    grad_down = mm(weighted, grads_all, 0, 0).astype(BF)

    gate_all, up_all = gate_all.astype(F32), up_all.astype(F32)
    sigma = jax.nn.sigmoid(gate_all)
    grad_gate_pre = (grad_hidden * up_all * sigma * (1.0 + gate_all * (1.0 - sigma))).astype(BF)
    grad_up_pre = (grad_hidden * gate_all * sigma).astype(BF)
    grad_gate = mm(arrived, grad_gate_pre, 0, 0).astype(BF)
    grad_up = mm(arrived, grad_up_pre, 0, 0).astype(BF)
    return (mixed, grad_gate[None], grad_up[None], grad_down[None])


def across(value):
    count = lax.axis_size("ep")
    return lax.ppermute(value, "ep", [(i, i ^ 1) for i in range(count)])


def same_core():
    count = lax.axis_size("ep")
    return [list(range(core, count, 2)) for core in range(2)]


def of_core(value, core, rows):
    count = value.shape[0] // rows
    value = value.reshape(count // 2, 2, rows, value.shape[1])
    picked = lax.dynamic_index_in_dim(value, core, 1, keepdims=False)
    return picked.reshape(count // 2 * rows, value.shape[3])


def local(signal, routes, gates, pairing, w_gate, w_up, w_down):
    experts = lax.axis_size("ep")
    rank = lax.axis_index("rep")
    core = lax.axis_index("ep") % 2
    row_count, width = signal.shape
    capacity = min(row_count, row_count * TOP * 5 // (4 * experts))
    w_gate, w_up, w_down = w_gate[0], w_up[0], w_down[0]
    hidden_width = w_gate.shape[1]
    group = experts // GROUPS
    spans = [(low, low + group) for low in range(0, experts, group)]

    rows_all = lax.all_gather(signal, "ep", axis=0, tiled=True)
    rows_all, w_down_other = lax.optimization_barrier((rows_all, across(w_down)))
    w_down_pair = jnp.concatenate([w_down, w_down_other], 0)
    w_both = jnp.concatenate([w_gate, w_up], 1)
    weight = gate_table(routes, gates, experts)
    pick = slot_picks(weight, capacity)
    row_weight = weight.reshape(experts * row_count, 1)

    arrived, gate_up, weighted, kept, handed = [], [], [], [], []
    for low, high in spans:
        count = high - low
        rows = rows_all[low * row_count : high * row_count]
        chosen = pick[low:high]
        arrived.append(
            blocks_mm(chosen, rows.reshape(count, row_count, width), 2, 1)
            .astype(BF)
            .reshape(count * capacity, width)
        )
        own = half_sum(mm(arrived[-1], w_both).astype(BF), rank)
        gate, up = own[:, :hidden_width], own[:, hidden_width:]
        hidden_own = (gate * jax.nn.sigmoid(gate) * up).astype(BF)
        gate_up.append(own.astype(BF))
        hidden = both_halves(hidden_own, swap(hidden_own), rank)
        spread = blocks_mm(chosen, hidden.reshape(count, capacity, hidden_width), 1, 1).reshape(
            count * row_count, hidden_width
        )
        weighted.append((spread * row_weight[low * row_count : high * row_count]).astype(BF))
        kept.append(of_core(weighted[-1], core, row_count))
        handed.append(across(of_core(weighted[-1], 1 - core, row_count)))

    inner = jnp.concatenate([jnp.concatenate(kept, 0), jnp.concatenate(handed, 0)], 1)
    returned = mm(inner, w_down_pair).astype(BF)
    combined = lax.psum_scatter(
        returned, "ep", scatter_dimension=0, tiled=True, axis_index_groups=same_core()
    )
    others = [swap(value) for value in gate_up]
    combined, others = lax.optimization_barrier((combined, others))
    mixed = combined
    grad_rows = row_gradient(combined.astype(F32), pairing)

    grads_all = lax.all_gather(grad_rows, "ep", axis=0, tiled=True)
    gate_pre, up_pre = [], []
    for (low, high), own, other in zip(spans, gate_up, others):
        count = high - low
        rows = grads_all[low * row_count : high * row_count]
        product = (mm(rows, w_down, 1, 1) * row_weight[low * row_count : high * row_count]).astype(BF)
        sent = (
            blocks_mm(pick[low:high], product.reshape(count, row_count, hidden_width), 2, 1)
            .reshape(count * capacity, hidden_width)
            .astype(BF)
        )
        grad_hidden = sent.astype(F32) + swap(sent).astype(F32)
        both = both_halves(own, other, rank).astype(F32)
        gate, up = both[:, :hidden_width], both[:, hidden_width:]
        sigma = jax.nn.sigmoid(gate)
        gate_pre.append(
            (grad_hidden * up * sigma * (1.0 + gate * (1.0 - sigma))).astype(BF)
        )
        up_pre.append((grad_hidden * gate * sigma).astype(BF))
    grad_down = mm(jnp.concatenate(weighted, 0), grads_all, 0, 0).astype(BF)
    arrived = jnp.concatenate(arrived, 0)
    grad_gate = mm(arrived, jnp.concatenate(gate_pre, 0), 0, 0).astype(BF)
    grad_up = mm(arrived, jnp.concatenate(up_pre, 0), 0, 0).astype(BF)
    return (mixed, grad_gate[None], grad_up[None], grad_down[None])


def solution(mesh):
    blocked = mesh.shape["ep"] % 4 == 0 and mesh.shape["rep"] == 2
    return jax.shard_map(
        local if blocked else local_general,
        mesh=mesh,
        in_specs=(
            P("ep", "rep"),
            P("ep", None),
            P("ep", None),
            P("ep"),
            P("ep", "rep", None),
            P("ep", "rep", None),
            P("ep", None, "rep"),
        ),
        out_specs=(
            P("ep", "rep"),
            P("ep", "rep", None),
            P("ep", "rep", None),
            P("ep", None, "rep"),
        ),
        check_vma=False,
    )
```
